256 devices in a mesh: layer: 32 (over x_hi, z, core), row: 8 (over x_lo, y).
Axes of the slice: x: 4 (x_hi: 2, x_lo: 2; x = x_hi * 2 + x_lo), y: 4, z: 8, core: 2. Of those that a mesh axis runs over, the one named last changes fastest.
Arguments:
- waves: bfloat16 [32, 3072, 512], P('layer', 'row'), may hold values from -6 to 6
- operators: bfloat16 [32, 4, 3072, 3072], P('layer', None, 'row'), may hold values from -0.0546875 to 0.0546875
- sources: bfloat16 [3072, 512], P('row'), may hold values from -6 to 6
- source_layer: int32 [128], replicated, may hold values from 0 to 31
Outputs:
- traces: bfloat16 [32, 3072, 512], P('layer', 'row')
The draws below stay inside these ranges and needn't reach their ends.
All inputs are finite; a program needn't handle non-finite values.
Results may differ from the reference program's by a relative error of at most 0.0057.
Values may be sent and summed in bfloat16 or wider, within the bound.
No kernel may reach another device: no remote copies, remote signals or barrier semaphores. Data moves between devices by JAX's collectives and lax.ppermute only.
A program may use at most 64 MiB of HBM per device.

```python
import jax
import jax.numpy as jnp
from jax import lax

M = 3072
C = 128
TICKS = 3
LAYERS = 32


def touch_ends(result, stream_key, least, top_value):
    place = [jax.random.randint(jax.random.fold_in(stream_key, axis), (), 0, length) for axis, length in enumerate(result.shape)]
    widest = result.shape.index(max(result.shape))
    next_to = place[:widest] + [(place[widest] + 1) % result.shape[widest]] + place[widest + 1:]
    return result.at[tuple(place)].set(least).at[tuple(next_to)].set(top_value)


def steps_of(stream_key, shape, shards, low, top_value):
    factor_of = 1.0
    for position, blocks in shards:
        steps = jax.random.uniform(jax.random.fold_in(jax.random.fold_in(stream_key, 6), position), (blocks,), jnp.float32, low / len(shards), top_value / len(shards))
        factor_of = factor_of * jnp.repeat(jnp.exp(steps), shape[position] // blocks).reshape((-1,) + (1,) * (len(shape) - 1 - position))
    return factor_of


def bell_draw(own_key, shape, scale, limit, cuts=(), kind=jnp.bfloat16):
    array = scale * jax.random.normal(own_key, shape, jnp.float32)
    if cuts:
        array = array * steps_of(own_key, shape, cuts, -0.22, 0.18)
    return jnp.clip(array, -limit, limit).astype(kind)


def setup_inputs(seed: int = 0) -> dict:
    key_list = jax.random.split(jax.random.key(seed), 5)
    waves = bell_draw(key_list[0], (LAYERS, M, 4 * C), 1.0, 6.0, ((0, 32), (1, 8)))
    operators = bell_draw(key_list[1], (LAYERS, 4, M, M), (4 * M) ** -0.5, 0.0546875, ((0, 32), (2, 8)))
    sources = bell_draw(key_list[2], (M, 4 * C), 1.0, 6.0, ((0, 8),))
    source_layer = touch_ends(jax.random.randint(key_list[3], (C,), 0, LAYERS), jax.random.fold_in(key_list[3], 1), 0, LAYERS - 1).astype(jnp.int32)
    return dict(waves=waves, operators=operators, sources=sources, source_layer=source_layer)


def combine(real_prod, imag_prod, shot_count):
    real_part = real_prod[:, :shot_count] - imag_prod[:, shot_count:]
    imag_part = real_prod[:, shot_count:] + imag_prod[:, :shot_count]
    return jnp.concatenate([real_part, imag_part], axis=1)


def layer_tick(operator_block, wave_block, layer_id, sources, source_layer):
    full_rows = operator_block.shape[1]
    products = jnp.dot(operator_block.reshape(4 * full_rows, full_rows), wave_block, preferred_element_type=jnp.float32)
    products = products.reshape(4, full_rows, 4 * C)
    half = 2 * C
    down_out = combine(products[0][:, :half], products[1][:, :half], C) + combine(products[2][:, half:], products[3][:, half:], C)
    up_out = combine(products[0][:, half:], products[1][:, half:], C) + combine(products[2][:, :half], products[3][:, :half], C)
    shot_mask = jnp.tile((source_layer == layer_id).astype(jnp.float32), 4)
    source_term = sources.astype(jnp.float32) * shot_mask[None, :]
    down_out = (down_out + source_term[:, :half]).astype(jnp.bfloat16)
    up_out = (up_out + source_term[:, half:]).astype(jnp.bfloat16)
    return down_out, up_out


def reference(waves, operators, sources, source_layer):
    current = waves
    layer_ids = jnp.arange(LAYERS).astype(jnp.int32)
    for sweep_tick in range(TICKS):
        downs, ups = lax.map(lambda packed: layer_tick(packed[0], packed[1], packed[2], sources, source_layer), (operators, current, layer_ids))
        empty_rim = jnp.zeros((1, M, 2 * C), jnp.bfloat16)
        new_down = jnp.concatenate([empty_rim, downs[:-1]], axis=0)
        new_up = jnp.concatenate([ups[1:], empty_rim], axis=0)
        current = jnp.concatenate([new_down, new_up], axis=2)
    return current
```

```python
import functools

import jax
import jax.numpy as jnp
from jax import lax
from jax.experimental import pallas as pl
from jax.experimental.pallas import tpu as pltpu
from jax.sharding import PartitionSpec as P

TICKS = 3
AXES = ("layer", "row")


def at_row(row, dx, dy):
    return ((row // 4 + dx) % 2) * 4 + (row % 4 + dy) % 4


def near_layer(layer):
    return layer ^ 1


def far_layer(layer):
    return layer - 1 if layer % 2 == 0 else layer + 1


def permute(array, layers, rows, layer_to, dx, dy):
    pairs = [
        (layer * rows + row, layer_to(layer) * rows + at_row(row, dx, dy))
        for layer in range(layers)
        for row in range(rows)
        if 0 <= layer_to(layer) < layers
    ]
    return lax.ppermute(array, AXES, pairs)


def block_product(op_buf, block, half):
    count = half // 2
    near_re, near_im = block[:, :count], block[:, count:half]
    far_re, far_im = block[:, half : half + count], block[:, half + count :]
    lhs = jnp.concatenate([op_buf[part] for part in range(4)], axis=1)
    rhs = jnp.concatenate(
        [
            jnp.concatenate([far_re, far_im, near_re, near_im], axis=1),
            jnp.concatenate([-far_im, far_re, -near_im, near_re], axis=1),
            jnp.concatenate([near_re, near_im, far_re, far_im], axis=1),
            jnp.concatenate([-near_im, near_re, -far_im, far_re], axis=1),
        ],
        axis=0,
    )
    return jnp.dot(lhs, rhs, preferred_element_type=jnp.float32)


def stage_kernel(layout, first, last, places, ops, *refs):
    refs = list(refs)
    count = sum(len(cols) for block in layout for cols in block)
    pieces, refs = refs[:count], refs[count:]
    extra = None
    if not first:
        before, refs = refs[0], refs[1:]
    if last:
        extra, refs = refs[0], refs[1:]
        near_out, far_out, op_buf, sems = refs
    else:
        total_out, op_buf, sems = refs
    rows = ops.shape[2]
    copies = []
    for j in range(len(layout)):
        copy = pltpu.make_async_copy(
            ops.at[0, :, :, pl.ds(pl.multiple_of(places[j] * rows, rows), rows)],
            op_buf.at[j],
            sems.at[j],
        )
        copy.start()
        copies.append(copy)
    total = None if first else before[...]
    at = 0
    for j, block in enumerate(layout):
        parts = []
        for cols in block:
            group = [pieces[at + c][...] for c in range(len(cols))]
            at += len(cols)
            parts.append(group[0] if len(group) == 1 else jnp.concatenate(group, axis=1))
        whole = parts[0] if len(parts) == 1 else jnp.concatenate(parts, axis=0)
        copies[j].wait()
        term = block_product(op_buf.at[j], whole, whole.shape[1] // 2)
        total = term if total is None else total + term
    if last:
        total = total + extra[...].astype(jnp.float32)
        half = total.shape[1] // 2
        near_out[...] = total[:, :half].astype(jnp.bfloat16)
        far_out[...] = total[:, half:].astype(jnp.bfloat16)
    else:
        total_out[...] = total


def stage(operators, places, blocks, before=None, extra=None):
    rows = operators.shape[2]
    layout = [[[0] * len(cols) for cols in block] for block in blocks]
    flat = [piece for block in blocks for cols in block for piece in cols]
    width = sum(piece.shape[1] for piece in blocks[0][0])
    operands = [places, operators] + flat
    if before is not None:
        operands.append(before)
    if extra is not None:
        operands.append(extra)
    vmem = pl.BlockSpec(memory_space=pltpu.VMEM)
    if extra is not None:
        out_shape = [jax.ShapeDtypeStruct((rows, width // 2), jnp.bfloat16)] * 2
        out_specs = [vmem, vmem]
    else:
        out_shape = jax.ShapeDtypeStruct((rows, width), jnp.float32)
        out_specs = vmem
    n = len(blocks)
    return pl.pallas_call(
        functools.partial(stage_kernel, layout, before is None, extra is not None),
        out_shape=out_shape,
        in_specs=[pl.BlockSpec(memory_space=pltpu.SMEM), pl.BlockSpec(memory_space=pl.ANY)]
        + [vmem] * (len(operands) - 2),
        out_specs=out_specs,
        scratch_shapes=[
            pltpu.VMEM((n, 4, rows, rows), jnp.bfloat16),
            pltpu.SemaphoreType.DMA((n,)),
        ],
        compiler_params=pltpu.CompilerParams(vmem_limit_bytes=24 * 2**20),
        cost_estimate=pl.CostEstimate(
            flops=2 * n * 4 * rows * rows * width,
            bytes_accessed=n * (4 * rows * rows + rows * width) * 2,
            transcendentals=0,
        ),
    )(*operands)


def per_device(layers, waves, operators, sources, source_layer):
    rows = 8
    tile_rows = operators.shape[2]
    half = waves.shape[2] // 2
    third = tile_rows // 3
    layer_id = lax.axis_index("layer")
    row_id = lax.axis_index("row")
    even = layer_id % 2 == 0

    def place(dx, dy):
        return at_row(row_id, dx, dy)

    def places(*shifts):
        return jnp.stack([place(dx, dy) for dx, dy in shifts]).astype(jnp.int32)

    def swap_if_even(array):
        swapped = jnp.concatenate([array[:, half:], array[:, :half]], axis=1)
        return jnp.where(even, swapped, array)

    def stay(layer):
        return layer

    def move(array, dx, dy):
        return permute(array, layers, rows, stay, dx, dy)

    mask = jnp.tile((source_layer == layer_id).astype(jnp.bfloat16), 4)
    masked = sources * mask[None, :]
    swapped = jnp.concatenate([masked[:, half:], masked[:, :half]], axis=1)
    source_term = jnp.where(even, masked, swapped)
    own = swap_if_even(waves[0])
    for tick in range(TICKS):
        below = move(own, 0, -1)
        above = move(own, 0, 1)
        across = move(own, 1, 0)
        far_y = move(below, 0, -1)
        across_above = move(across, 0, 1)
        across_below = move(below, 1, 0)
        part0 = move(far_y[:third], 1, 0)
        part1 = move(across_above[third : 2 * third], 0, 1)
        part2 = move(across_below[2 * third :], 0, -1)
        total = stage(
            operators, places((0, 0), (0, 1), (0, -1), (1, 0)), [[[own]], [[below]], [[above]], [[across]]]
        )
        total = stage(
            operators,
            places((0, 2), (1, -1), (1, 1)),
            [[[far_y]], [[across_above]], [[across_below]]],
            before=total,
        )
        near, far = stage(
            operators, places((1, 2)), [[[part0], [part1], [part2]]], before=total, extra=source_term
        )
        near_in = permute(near, layers, rows, near_layer, 0, 0)
        far_in = permute(far, layers, rows, far_layer, 0, 0)
        own = jnp.concatenate([near_in, far_in], axis=1)
    return swap_if_even(own)[None]


def solution(mesh):
    return jax.shard_map(
        functools.partial(per_device, mesh.shape["layer"]),
        mesh=mesh,
        in_specs=(P("layer", "row", None), P("layer", None, "row", None), P("row", None), P()),
        out_specs=P("layer", "row", None),
        check_vma=False,
    )
```

```python
import functools

import jax
import jax.numpy as jnp
from jax import lax
from jax.experimental import pallas as pl
from jax.experimental.pallas import tpu as pltpu
from jax.sharding import PartitionSpec as P

TICKS = 3
AXES = ("layer", "row")
VMEM = pl.BlockSpec(memory_space=pltpu.VMEM)
SMEM = pl.BlockSpec(memory_space=pltpu.SMEM)
HBM = pl.BlockSpec(memory_space=pltpu.HBM)


def at_row(row, dx, dy):
    return (row ^ (4 * dx)) & 4 | (row + dy) & 3


def stay(layer):
    return layer


def near_layer(layer):
    return layer ^ 1


def far_layer(layer):
    return layer - 1 if layer % 2 == 0 else layer + 1


def permute(array, layers, rows, layer_to, dx, dy):
    pairs = [
        (layer * rows + row, layer_to(layer) * rows + at_row(row, dx, dy))
        for layer in range(layers)
        for row in range(rows)
        if 0 <= layer_to(layer) < layers
    ]
    return lax.ppermute(array, AXES, pairs)


def block_product(ops, near, far):
    count = near.shape[1] // 2
    near_re, near_im, far_re, far_im = near[:, :count], near[:, count:], far[:, :count], far[:, count:]
    lhs = jnp.concatenate([ops[part] for part in range(4)], axis=1)
    rhs = jnp.concatenate(
        [
            jnp.concatenate([far_re, far_im, near_re, near_im], axis=1),
            jnp.concatenate([-far_im, far_re, -near_im, near_re], axis=1),
            jnp.concatenate([near_re, near_im, far_re, far_im], axis=1),
            jnp.concatenate([-near_im, near_re, -far_im, far_re], axis=1),
        ],
        axis=0,
    )
    return jnp.dot(lhs, rhs, preferred_element_type=jnp.float32)


def halves_of(refs, swap):
    if len(refs) == 2:
        return refs[0][...], refs[1][...]
    half = refs[0].shape[1] // 2
    first, second = refs[0][:, :half], refs[0][:, half:]
    if swap is None:
        return first, second
    return jnp.where(swap, second, first), jnp.where(swap, first, second)


def stage_kernel(shifts, layout, parity, first, last, where, ops, *refs):
    refs = list(refs)
    blocks = []
    for parts in layout:
        blocks.append([])
        for count in parts:
            blocks[-1].append(refs[:count])
            refs = refs[count:]
    if not first:
        before, refs = refs[0], refs[1:]
    if last:
        sources, source_layer, near_out, far_out, op_buf, sems = refs
    else:
        total_out, op_buf, sems = refs
    rows = ops.shape[2]
    even = where[1] % 2 == 0
    copies = []
    for j, shift in enumerate(shifts):
        place = at_row(where[0], *shift)
        copy = pltpu.make_async_copy(
            ops.at[0, :, :, pl.ds(pl.multiple_of(place * rows, rows), rows)], op_buf.at[j], sems.at[j]
        )
        copy.start()
        copies.append(copy)
    total = None if first else before[...]
    for j, parts in enumerate(blocks):
        halves = [halves_of(part, even if parity else None) for part in parts]
        near, far = (jnp.concatenate(half, axis=0) for half in zip(*halves))
        copies[j].wait()
        term = block_product(op_buf.at[j], near, far)
        total = term if total is None else total + term
    if last:
        half = total.shape[1] // 2
        mask = (source_layer[...] == where[1]).astype(jnp.float32)
        mask = jnp.concatenate([mask, mask], axis=1)
        down, up = sources[:, :half].astype(jnp.float32) * mask, sources[:, half:].astype(jnp.float32) * mask
        near_out[...] = (total[:, :half] + jnp.where(even, down, up)).astype(jnp.bfloat16)
        far_out[...] = (total[:, half:] + jnp.where(even, up, down)).astype(jnp.bfloat16)
    else:
        total_out[...] = total


def stage(operators, where, blocks, parity=False, before=None, extra=None):
    rows = operators.shape[2]
    shifts = [shift for shift, _ in blocks]
    layout = [[len(part) for part in parts] for _, parts in blocks]
    flat = [array for _, parts in blocks for part in parts for array in part]
    width = sum(array.shape[1] for array in blocks[0][1][0])
    operands = [where, operators] + flat
    if before is not None:
        operands.append(before)
    if extra is not None:
        operands.extend(extra)
        out_shape = [jax.ShapeDtypeStruct((rows, width // 2), jnp.bfloat16)] * 2
        out_specs = [VMEM, VMEM]
    else:
        out_shape = jax.ShapeDtypeStruct((rows, width), jnp.float32)
        out_specs = VMEM
    n = len(blocks)
    return pl.pallas_call(
        functools.partial(stage_kernel, shifts, layout, parity, before is None, extra is not None),
        out_shape=out_shape,
        in_specs=[SMEM, HBM] + [VMEM] * (len(operands) - 2),
        out_specs=out_specs,
        scratch_shapes=[
            pltpu.VMEM((n, 4, rows, rows), jnp.bfloat16),
            pltpu.SemaphoreType.DMA((n,)),
        ],
        compiler_params=pltpu.CompilerParams(vmem_limit_bytes=48 * 2**20),
        cost_estimate=pl.CostEstimate(
            flops=2 * n * 4 * rows * rows * width,
            bytes_accessed=n * (4 * rows * rows + rows * width) * 2,
            transcendentals=0,
        ),
    )(*operands)


def join_kernel(near, far, out):
    half = near.shape[1]
    out[:, :half] = near[...]
    out[:, half:] = far[...]


def join(near, far):
    return pl.pallas_call(
        join_kernel,
        out_shape=jax.ShapeDtypeStruct((near.shape[0], 2 * near.shape[1]), near.dtype),
        in_specs=[VMEM, VMEM],
        out_specs=VMEM,
        compiler_params=pltpu.CompilerParams(vmem_limit_bytes=2 * 2**20),
    )(near, far)


def finish_kernel(where, near, far, out):
    half = near.shape[1]
    even = where[1] % 2 == 0
    out[0, :, :half] = jnp.where(even, far[...], near[...])
    out[0, :, half:] = jnp.where(even, near[...], far[...])


def finish(where, near, far):
    return pl.pallas_call(
        finish_kernel,
        out_shape=jax.ShapeDtypeStruct((1, near.shape[0], 2 * near.shape[1]), near.dtype),
        in_specs=[SMEM, VMEM, VMEM],
        out_specs=VMEM,
        compiler_params=pltpu.CompilerParams(vmem_limit_bytes=2 * 2**20),
    )(where, near, far)


def per_device(layers, rows, waves, operators, sources, source_layer):
    third = operators.shape[2] // 3
    where = jnp.stack([lax.axis_index("row"), lax.axis_index("layer")]).astype(jnp.int32)
    source_layer = source_layer.reshape(1, -1)

    def move(array, dx, dy):
        return permute(array, layers, rows, stay, dx, dy)

    outs = None
    for tick in range(TICKS):
        if outs is None:
            own = [waves[0]]
            below, across, above = [move(own[0], 0, -1)], [move(own[0], 1, 0)], [move(own[0], 0, 1)]
            below_whole, across_whole = below[0], across[0]
        else:
            targets = ((0, -1), (1, 0), (0, 1), (0, 0))
            below, across, above, own = (
                [permute(out, layers, rows, to, *shift) for out, to in zip(outs, (near_layer, far_layer))]
                for shift in targets
            )
            below_whole, across_whole = join(*below), join(*across)
        far_y = move(below_whole, 0, -1)
        across_below = move(below_whole, 1, 0)
        across_above = move(across_whole, 0, 1)
        part0 = move(far_y[:third], 1, 0)
        part1 = move(across_above[third : 2 * third], 0, 1)
        part2 = move(across_below[2 * third :], 0, -1)
        total = stage(
            operators,
            where,
            [((0, 0), [own]), ((0, 1), [below]), ((1, 0), [across]), ((0, -1), [above])],
            parity=tick == 0,
        )
        total = stage(
            operators,
            where,
            [((0, 2), [[far_y]]), ((1, 1), [[across_below]]), ((1, -1), [[across_above]])],
            parity=tick == 0,
            before=total,
        )
        outs = stage(
            operators,
            where,
            [((1, 2), [[part0], [part1], [part2]])],
            parity=tick == 0,
            before=total,
            extra=(sources, source_layer),
        )
    near_in = permute(outs[0], layers, rows, near_layer, 0, 0)
    far_in = permute(outs[1], layers, rows, far_layer, 0, 0)
    return finish(where, near_in, far_in)


def solution(mesh):
    return jax.shard_map(
        functools.partial(per_device, mesh.shape["layer"], mesh.shape["row"]),
        mesh=mesh,
        in_specs=(P("layer", "row", None), P("layer", None, "row", None), P("row", None), P()),
        out_specs=P("layer", "row", None),
        check_vma=False,
    )
```

```python
import functools

import jax
import jax.numpy as jnp
from jax import lax
from jax.experimental import pallas as pl
from jax.experimental.pallas import tpu as pltpu
from jax.sharding import PartitionSpec as P

TICKS = 3
AXES = ("layer", "row")
VMEM = pl.BlockSpec(memory_space=pltpu.VMEM)
SMEM = pl.BlockSpec(memory_space=pltpu.SMEM)


def at_row(row, dx, dy):
    return (row ^ (4 * dx)) & 4 | (row + dy) & 3


def stay(layer):
    return layer


def near_layer(layer):
    return layer ^ 1


def far_layer(layer):
    return layer - 1 if layer % 2 == 0 else layer + 1


def permute(array, layers, rows, layer_to, dx, dy):
    pairs = [
        (layer * rows + row, layer_to(layer) * rows + at_row(row, dx, dy))
        for layer in range(layers)
        for row in range(rows)
        if 0 <= layer_to(layer) < layers
    ]
    return lax.ppermute(array, AXES, pairs)


def block_product(ops, block):
    count = block.shape[1] // 4
    re1, im1, re2, im2 = (block[:, j * count : (j + 1) * count] for j in range(4))
    lhs = jnp.concatenate(ops, axis=1)
    rhs = jnp.concatenate(
        [
            block,
            jnp.concatenate([-im1, re1, -im2, re2], axis=1),
            jnp.concatenate([re2, im2, re1, im1], axis=1),
            jnp.concatenate([-im2, re2, -im1, re1], axis=1),
        ],
        axis=0,
    )
    return jnp.dot(lhs, rhs, preferred_element_type=jnp.float32)


def stage_kernel(shifts, layout, parity, first, last, where, ops, *refs):
    refs = list(refs)
    blocks = []
    for parts in layout:
        blocks.append([])
        for count in parts:
            blocks[-1].append(refs[:count])
            refs = refs[count:]
    if not first:
        before, refs = refs[0], refs[1:]
    if last:
        extra, near_out, far_out = refs
    else:
        (total_out,) = refs
    rows = ops.shape[2]
    total = None if first else before[...]
    for j, parts in enumerate(blocks):
        whole = [jnp.concatenate([ref[...] for ref in part], axis=1) for part in parts]
        block = jnp.concatenate(whole, axis=0)
        place = at_row(where[0], *shifts[j])
        columns = pl.ds(pl.multiple_of(place * rows, rows), rows)
        term = block_product([ops[0, part, :, columns] for part in range(4)], block)
        total = term if total is None else total + term
    if last:
        half = total.shape[1] // 2
        near, far = total[:, half:], total[:, :half]
        if parity:
            even = where[1] % 2 == 0
            near, far = jnp.where(even, far, near), jnp.where(even, near, far)
        near_out[...] = (near + extra[:, :half].astype(jnp.float32)).astype(jnp.bfloat16)
        far_out[...] = (far + extra[:, half:].astype(jnp.float32)).astype(jnp.bfloat16)
    else:
        total_out[...] = total


def stage(operators, where, blocks, parity=False, before=None, extra=None):
    rows = operators.shape[2]
    shifts = [shift for shift, _ in blocks]
    layout = [[len(part) for part in parts] for _, parts in blocks]
    flat = [array for _, parts in blocks for part in parts for array in part]
    width = sum(array.shape[1] for array in blocks[0][1][0])
    operands = [where, operators] + flat
    if before is not None:
        operands.append(before)
    if extra is not None:
        operands.append(extra)
        out_shape = [jax.ShapeDtypeStruct((rows, width // 2), jnp.bfloat16)] * 2
        out_specs = [VMEM, VMEM]
    else:
        out_shape = jax.ShapeDtypeStruct((rows, width), jnp.float32)
        out_specs = VMEM
    n = len(blocks)
    return pl.pallas_call(
        functools.partial(stage_kernel, shifts, layout, parity, before is None, extra is not None),
        out_shape=out_shape,
        in_specs=[SMEM] + [VMEM] * (len(operands) - 1),
        out_specs=out_specs,
        compiler_params=pltpu.CompilerParams(vmem_limit_bytes=24 * 2**20),
        cost_estimate=pl.CostEstimate(
            flops=2 * n * 4 * rows * rows * width,
            bytes_accessed=n * (4 * rows * rows + rows * width) * 2,
            transcendentals=0,
        ),
    )(*operands)


def sources_kernel(where, sources, source_layer, out):
    half = sources.shape[1] // 2
    mask = source_layer[...] == where[1]
    mask = jnp.concatenate([mask, mask], axis=1)
    down = jnp.where(mask, sources[:, :half].astype(jnp.float32), 0.0)
    up = jnp.where(mask, sources[:, half:].astype(jnp.float32), 0.0)
    even = where[1] % 2 == 0
    out[:, :half] = jnp.where(even, down, up).astype(jnp.bfloat16)
    out[:, half:] = jnp.where(even, up, down).astype(jnp.bfloat16)


def layer_sources(where, sources, source_layer):
    return pl.pallas_call(
        sources_kernel,
        out_shape=jax.ShapeDtypeStruct(sources.shape, jnp.bfloat16),
        in_specs=[SMEM, VMEM, VMEM],
        out_specs=VMEM,
        compiler_params=pltpu.CompilerParams(vmem_limit_bytes=6 * 2**20),
    )(where, sources, source_layer)


def per_device(layers, rows, waves, operators, sources, source_layer):
    third = operators.shape[2] // 3
    where = jnp.stack([lax.axis_index("row"), lax.axis_index("layer")]).astype(jnp.int32)

    def move(array, dx, dy):
        return permute(array, layers, rows, stay, dx, dy)

    outs = None
    for tick in range(TICKS):
        if outs is None:
            own = [waves[0]]
        else:
            own = [jnp.concatenate([near_in, far_in], axis=1)]
        below, across, above = move(own[0], 0, -1), move(own[0], 1, 0), move(own[0], 0, 1)
        total = stage(operators, where, [((0, 0), [own])])
        if tick == 0:
            source_term = layer_sources(where, sources, source_layer.reshape(1, -1))
            below, across, total, source_term = lax.optimization_barrier((below, across, total, source_term))
        far_y = move(below, 0, -1)
        across_below = move(below, 1, 0)
        across_above = move(across, 0, 1)
        part0 = move(far_y[:third], 1, 0)
        part1 = move(across_above[third : 2 * third], 0, 1)
        part2 = move(across_below[2 * third :], 0, -1)
        total = stage(
            operators, where, [((0, 1), [[below]]), ((1, 0), [[across]]), ((0, -1), [[above]])], before=total
        )
        total = stage(
            operators,
            where,
            [((0, 2), [[far_y]]), ((1, 1), [[across_below]]), ((1, -1), [[across_above]])],
            before=total,
        )
        outs = stage(
            operators,
            where,
            [((1, 2), [[part0], [part1], [part2]])],
            parity=tick == 0,
            before=total,
            extra=source_term,
        )
        near_in = permute(outs[0], layers, rows, near_layer, 0, 0)
        far_in = permute(outs[1], layers, rows, far_layer, 0, 0)
    even = where[1] % 2 == 0
    down, up = jnp.where(even, far_in, near_in), jnp.where(even, near_in, far_in)
    return jnp.concatenate([down, up], axis=1)[None]


def solution(mesh):
    return jax.shard_map(
        functools.partial(per_device, mesh.shape["layer"], mesh.shape["row"]),
        mesh=mesh,
        in_specs=(P("layer", "row", None), P("layer", None, "row", None), P("row", None), P()),
        out_specs=P("layer", "row", None),
        check_vma=False,
    )
```

```python
import functools

import jax
import jax.numpy as jnp
from jax import lax
from jax.experimental import pallas as pl
from jax.experimental.pallas import tpu as pltpu
from jax.sharding import PartitionSpec as P

TICKS = 3
AXES = ("layer", "row")
VMEM = pl.BlockSpec(memory_space=pltpu.VMEM)
SMEM = pl.BlockSpec(memory_space=pltpu.SMEM)


def at_row(row, dx, dy):
    return (row ^ (4 * dx)) & 4 | (row + dy) & 3


def stay(layer):
    return layer


def near_layer(layer):
    return layer ^ 1


def far_layer(layer):
    return layer - 1 if layer % 2 == 0 else layer + 1


def permute(array, layers, rows, layer_to, dx, dy):
    pairs = [
        (layer * rows + row, layer_to(layer) * rows + at_row(row, dx, dy))
        for layer in range(layers)
        for row in range(rows)
        if 0 <= layer_to(layer) < layers
    ]
    return lax.ppermute(array, AXES, pairs)


def block_product(ops, block):
    count = block.shape[1] // 4
    re1, im1, re2, im2 = (block[:, j * count : (j + 1) * count] for j in range(4))
    lhs = jnp.concatenate(ops, axis=1)
    rhs = jnp.concatenate(
        [
            block,
            jnp.concatenate([-im1, re1, -im2, re2], axis=1),
            jnp.concatenate([re2, im2, re1, im1], axis=1),
            jnp.concatenate([-im2, re2, -im1, re1], axis=1),
        ],
        axis=0,
    )
    return jnp.dot(lhs, rhs, preferred_element_type=jnp.float32)


def stage_kernel(shifts, layout, parity, first, last, where, ops, *refs):
    refs = list(refs)
    blocks = []
    for parts in layout:
        blocks.append([])
        for count in parts:
            blocks[-1].append(refs[:count])
            refs = refs[count:]
    if not first:
        before, refs = refs[0], refs[1:]
    if last:
        extra, near_out, far_out = refs
    else:
        (total_out,) = refs
    rows = ops.shape[2]
    total = None if first else before[...]
    for j, parts in enumerate(blocks):
        whole = [jnp.concatenate([ref[...] for ref in part], axis=1) for part in parts]
        block = jnp.concatenate(whole, axis=0)
        place = at_row(where[0], *shifts[j])
        columns = pl.ds(pl.multiple_of(place * rows, rows), rows)
        term = block_product([ops[0, part, :, columns] for part in range(4)], block)
        total = term if total is None else total + term
    if last:
        half = total.shape[1] // 2
        near, far = total[:, half:], total[:, :half]
        if parity:
            even = where[1] % 2 == 0
            near, far = jnp.where(even, far, near), jnp.where(even, near, far)
        near_out[...] = (near + extra[:, :half].astype(jnp.float32)).astype(jnp.bfloat16)
        far_out[...] = (far + extra[:, half:].astype(jnp.float32)).astype(jnp.bfloat16)
    else:
        total_out[...] = total


def stage(operators, where, blocks, parity=False, before=None, extra=None):
    rows = operators.shape[2]
    shifts = [shift for shift, _ in blocks]
    layout = [[len(part) for part in parts] for _, parts in blocks]
    flat = [array for _, parts in blocks for part in parts for array in part]
    width = sum(array.shape[1] for array in blocks[0][1][0])
    operands = [where, operators] + flat
    if before is not None:
        operands.append(before)
    if extra is not None:
        operands.append(extra)
        out_shape = [jax.ShapeDtypeStruct((rows, width // 2), jnp.bfloat16)] * 2
        out_specs = [VMEM, VMEM]
    else:
        out_shape = jax.ShapeDtypeStruct((rows, width), jnp.float32)
        out_specs = VMEM
    n = len(blocks)
    return pl.pallas_call(
        functools.partial(stage_kernel, shifts, layout, parity, before is None, extra is not None),
        out_shape=out_shape,
        in_specs=[SMEM] + [VMEM] * (len(operands) - 1),
        out_specs=out_specs,
        compiler_params=pltpu.CompilerParams(vmem_limit_bytes=24 * 2**20),
        cost_estimate=pl.CostEstimate(
            flops=2 * n * 4 * rows * rows * width,
            bytes_accessed=n * (4 * rows * rows + rows * width) * 2,
            transcendentals=0,
        ),
    )(*operands)


def sources_kernel(where, sources, source_layer, out):
    half = sources.shape[1] // 2
    mask = source_layer[...] == where[1]
    mask = jnp.concatenate([mask, mask], axis=1)
    down = jnp.where(mask, sources[:, :half].astype(jnp.float32), 0.0)
    up = jnp.where(mask, sources[:, half:].astype(jnp.float32), 0.0)
    even = where[1] % 2 == 0
    out[:, :half] = jnp.where(even, down, up).astype(jnp.bfloat16)
    out[:, half:] = jnp.where(even, up, down).astype(jnp.bfloat16)


def layer_sources(where, sources, source_layer):
    return pl.pallas_call(
        sources_kernel,
        out_shape=jax.ShapeDtypeStruct(sources.shape, jnp.bfloat16),
        in_specs=[SMEM, VMEM, VMEM],
        out_specs=VMEM,
        compiler_params=pltpu.CompilerParams(vmem_limit_bytes=6 * 2**20),
    )(where, sources, source_layer)


def per_device(layers, rows, waves, operators, sources, source_layer):
    half = operators.shape[2] // 2
    where = jnp.stack([lax.axis_index("row"), lax.axis_index("layer")]).astype(jnp.int32)

    def move(array, dx, dy):
        return permute(array, layers, rows, stay, dx, dy)

    outs = None
    for tick in range(TICKS):
        if outs is None:
            own = [waves[0]]
        else:
            own = [jnp.concatenate([near_in, far_in], axis=1)]
        below, across, above = move(own[0], 0, -1), move(own[0], 1, 0), move(own[0], 0, 1)
        total = stage(operators, where, [((0, 0), [own])])
        if tick == 0:
            source_term = layer_sources(where, sources, source_layer.reshape(1, -1))
            below, across, total, source_term = lax.optimization_barrier((below, across, total, source_term))
        far_y = [move(below[:half], 0, -1), move(below[half:], 0, -1)]
        across_above = [move(across[:half], 0, 1), move(across[half:], 0, 1)]
        across_below = move(below, 1, 0)
        opposite = [move(far_y[0], 1, 0), move(across_above[1], 0, 1)]
        total = stage(
            operators, where, [((0, 1), [[below]]), ((1, 0), [[across]]), ((0, -1), [[above]])], before=total
        )
        total = stage(
            operators,
            where,
            [
                ((0, 2), [[part] for part in far_y]),
                ((1, -1), [[part] for part in across_above]),
                ((1, 1), [[across_below]]),
            ],
            before=total,
        )
        outs = stage(
            operators,
            where,
            [((1, 2), [[part] for part in opposite])],
            parity=tick == 0,
            before=total,
            extra=source_term,
        )
        near_in = permute(outs[0], layers, rows, near_layer, 0, 0)
        far_in = permute(outs[1], layers, rows, far_layer, 0, 0)
    even = where[1] % 2 == 0
    down, up = jnp.where(even, far_in, near_in), jnp.where(even, near_in, far_in)
    return jnp.concatenate([down, up], axis=1)[None]


def solution(mesh):
    return jax.shard_map(
        functools.partial(per_device, mesh.shape["layer"], mesh.shape["row"]),
        mesh=mesh,
        in_specs=(P("layer", "row", None), P("layer", None, "row", None), P("row", None), P()),
        out_specs=P("layer", "row", None),
        check_vma=False,
    )
```

```python
import functools

import jax
import jax.numpy as jnp
from jax import lax
from jax.experimental import pallas as pl
from jax.experimental.pallas import tpu as pltpu
from jax.sharding import PartitionSpec as P

TICKS = 3
AXES = ("layer", "row")
VMEM = pl.BlockSpec(memory_space=pltpu.VMEM)
SMEM = pl.BlockSpec(memory_space=pltpu.SMEM)


def at_row(row, dx, dy):
    return (row ^ (4 * dx)) & 4 | (row + dy) & 3


def stay(layer):
    return layer


def near_layer(layer):
    return layer ^ 1


def far_layer(layer):
    return layer - 1 if layer % 2 == 0 else layer + 1


def permute(array, layers, rows, layer_to, dx, dy):
    pairs = [
        (layer * rows + row, layer_to(layer) * rows + at_row(row, dx, dy))
        for layer in range(layers)
        for row in range(rows)
        if 0 <= layer_to(layer) < layers
    ]
    return lax.ppermute(array, AXES, pairs)


def block_product(ops, block):
    count = block.shape[1] // 4
    re1, im1, re2, im2 = (block[:, j * count : (j + 1) * count] for j in range(4))
    lhs = jnp.concatenate(ops, axis=1)
    rhs = jnp.concatenate(
        [
            block,
            jnp.concatenate([-im1, re1, -im2, re2], axis=1),
            jnp.concatenate([re2, im2, re1, im1], axis=1),
            jnp.concatenate([-im2, re2, -im1, re1], axis=1),
        ],
        axis=0,
    )
    return jnp.dot(lhs, rhs, preferred_element_type=jnp.float32)


def stage_kernel(shifts, layout, parity, first, last, where, ops, *refs):
    refs = list(refs)
    blocks = []
    for parts in layout:
        blocks.append([])
        for count in parts:
            blocks[-1].append(refs[:count])
            refs = refs[count:]
    if not first:
        before, refs = refs[0], refs[1:]
    if last:
        extra, near_out, far_out = refs
    else:
        (total_out,) = refs
    rows = ops.shape[2]
    total = None if first else before[...]
    for j, parts in enumerate(blocks):
        whole = [jnp.concatenate([ref[...] for ref in part], axis=1) for part in parts]
        block = jnp.concatenate(whole, axis=0)
        place = at_row(where[0], *shifts[j])
        columns = pl.ds(pl.multiple_of(place * rows, rows), rows)
        term = block_product([ops[0, part, :, columns] for part in range(4)], block)
        total = term if total is None else total + term
    if last:
        half = total.shape[1] // 2
        near, far = total[:, half:], total[:, :half]
        if parity:
            even = where[1] % 2 == 0
            near, far = jnp.where(even, far, near), jnp.where(even, near, far)
        near_out[...] = (near + extra[:, :half].astype(jnp.float32)).astype(jnp.bfloat16)
        far_out[...] = (far + extra[:, half:].astype(jnp.float32)).astype(jnp.bfloat16)
    else:
        total_out[...] = total


def stage(operators, where, blocks, parity=False, before=None, extra=None):
    rows = operators.shape[2]
    shifts = [shift for shift, _ in blocks]
    layout = [[len(part) for part in parts] for _, parts in blocks]
    flat = [array for _, parts in blocks for part in parts for array in part]
    width = sum(array.shape[1] for array in blocks[0][1][0])
    operands = [where, operators] + flat
    if before is not None:
        operands.append(before)
    if extra is not None:
        operands.append(extra)
        out_shape = [jax.ShapeDtypeStruct((rows, width // 2), jnp.bfloat16)] * 2
        out_specs = [VMEM, VMEM]
    else:
        out_shape = jax.ShapeDtypeStruct((rows, width), jnp.float32)
        out_specs = VMEM
    n = len(blocks)
    return pl.pallas_call(
        functools.partial(stage_kernel, shifts, layout, parity, before is None, extra is not None),
        out_shape=out_shape,
        in_specs=[SMEM] + [VMEM] * (len(operands) - 1),
        out_specs=out_specs,
        compiler_params=pltpu.CompilerParams(vmem_limit_bytes=24 * 2**20),
        cost_estimate=pl.CostEstimate(
            flops=2 * n * 4 * rows * rows * width,
            bytes_accessed=n * (4 * rows * rows + rows * width) * 2,
            transcendentals=0,
        ),
    )(*operands)


def sources_kernel(where, sources, source_layer, out):
    half = sources.shape[1] // 2
    mask = source_layer[...] == where[1]
    mask = jnp.concatenate([mask, mask], axis=1)
    down = jnp.where(mask, sources[:, :half].astype(jnp.float32), 0.0)
    up = jnp.where(mask, sources[:, half:].astype(jnp.float32), 0.0)
    even = where[1] % 2 == 0
    out[:, :half] = jnp.where(even, down, up).astype(jnp.bfloat16)
    out[:, half:] = jnp.where(even, up, down).astype(jnp.bfloat16)


def layer_sources(where, sources, source_layer):
    return pl.pallas_call(
        sources_kernel,
        out_shape=jax.ShapeDtypeStruct(sources.shape, jnp.bfloat16),
        in_specs=[SMEM, VMEM, VMEM],
        out_specs=VMEM,
        compiler_params=pltpu.CompilerParams(vmem_limit_bytes=6 * 2**20),
    )(where, sources, source_layer)


def per_device(layers, rows, waves, operators, sources, source_layer):
    half = operators.shape[2] // 2
    where = jnp.stack([lax.axis_index("row"), lax.axis_index("layer")]).astype(jnp.int32)

    def move(array, dx, dy):
        return permute(array, layers, rows, stay, dx, dy)

    outs = None
    for tick in range(TICKS):
        if outs is None:
            own = [waves[0]]
        else:
            own = [jnp.concatenate([near_in, far_in], axis=1)]
        below, across, above = move(own[0], 0, -1), move(own[0], 1, 0), move(own[0], 0, 1)
        total = stage(operators, where, [((0, 0), [own])])
        if tick == 0:
            source_term = layer_sources(where, sources, source_layer.reshape(1, -1))
        below, across, total, source_term = lax.optimization_barrier((below, across, total, source_term))
        far_y = [move(below[:half], 0, -1), move(below[half:], 0, -1)]
        across_above = [move(across[:half], 0, 1), move(across[half:], 0, 1)]
        across_below = move(below, 1, 0)
        opposite = [move(far_y[0], 1, 0), move(across_above[1], 0, 1)]
        total = stage(
            operators, where, [((0, 1), [[below]]), ((1, 0), [[across]]), ((0, -1), [[above]])], before=total
        )
        total = stage(
            operators,
            where,
            [
                ((0, 2), [[part] for part in far_y]),
                ((1, -1), [[part] for part in across_above]),
                ((1, 1), [[across_below]]),
            ],
            before=total,
        )
        outs = stage(
            operators,
            where,
            [((1, 2), [[part] for part in opposite])],
            parity=tick == 0,
            before=total,
            extra=source_term,
        )
        near_in = permute(outs[0], layers, rows, near_layer, 0, 0)
        far_in = permute(outs[1], layers, rows, far_layer, 0, 0)
    even = where[1] % 2 == 0
    down, up = jnp.where(even, far_in, near_in), jnp.where(even, near_in, far_in)
    return jnp.concatenate([down, up], axis=1)[None]


def solution(mesh):
    return jax.shard_map(
        functools.partial(per_device, mesh.shape["layer"], mesh.shape["row"]),
        mesh=mesh,
        in_specs=(P("layer", "row", None), P("layer", None, "row", None), P("row", None), P()),
        out_specs=P("layer", "row", None),
        check_vma=False,
    )
```
